128 devices in a mesh: section: 8 (over x, y_lo), expert: 16 (over y_hi, z, core).
Axes of the slice: x: 4, y: 4 (y_hi: 2, y_lo: 2; y = y_hi * 2 + y_lo), z: 4, core: 2. Of those that a mesh axis runs over, the one named last changes fastest.
Arguments:
- up_acts: bfloat16 [8, 1024, 3584], P('section', 'expert'), may hold values from -6 to 6
- down_acts: bfloat16 [8, 1024, 3584], P('section', 'expert'), may hold values from -6 to 6
- norm_gain: float32 [8, 3584], P('section'), may hold values from 0.1 to 1.9
- up_routes: int32 [8, 1024, 2], P('section', 'expert'), may hold values from 0 to 3, all different within a row; in each aligned block of 64 rows (0 to 63, 64 to 127, ..., all dimensions but the last counted through in order) at most 64 rows name the same one
- down_routes: int32 [8, 1024, 2], P('section', 'expert'), may hold values from 0 to 3, all different within a row; in each aligned block of 64 rows (0 to 63, 64 to 127, ..., all dimensions but the last counted through in order) at most 64 rows name the same one
- up_gates: float32 [8, 1024, 2], P('section', 'expert'), may hold values from 0.2 to 1
- down_gates: float32 [8, 1024, 2], P('section', 'expert'), may hold values from 0.2 to 1
- gate_weight: bfloat16 [8, 3584, 8192], P('section', None, 'expert'), may hold values from -0.09375 to 0.09375
- up_weight: bfloat16 [8, 3584, 8192], P('section', None, 'expert'), may hold values from -0.09375 to 0.09375
- down_weight: bfloat16 [8, 8192, 3584], P('section', 'expert'), may hold values from -0.125 to 0.125
Outputs:
- next_up: bfloat16 [8, 1024, 3584], P('section', 'expert')
- next_down: bfloat16 [8, 1024, 3584], P('section', 'expert')
The draws below stay inside these ranges and needn't reach their ends.
Inputs may be any that keep to these rules, and one draw needn't show every extreme that they name: `up_routes`: each row names 2 different experts. `down_routes`: each row names 2 different experts.
All inputs are finite; a program needn't handle non-finite values.
Results may differ from the reference program's by a relative error of at most 0.0052.
Values may be sent and summed in bfloat16 or wider, within the bound.
No kernel may reach another device: no remote copies, remote signals or barrier semaphores. Data moves between devices by JAX's collectives and lax.ppermute only.
A program may use at most 128 MiB of HBM per device.

```python
import math
import jax
import jax.numpy as jnp
import numpy as np
from jax import lax

D = 3584
FF = 2048
TOPK = 2
TOK_DEV = 64
SPLIT = 4
H_DEV = 512
EXPERTS = 4
TOKS = 1024
SECTIONS = 8


def steps_of(rng, extent, pieces, least, high):
    loudness = 1.0
    for dim, shards_of in pieces:
        steps = jax.random.uniform(jax.random.fold_in(jax.random.fold_in(rng, 6), dim), (shards_of,), jnp.float32, least / len(pieces), high / len(pieces))
        loudness = loudness * jnp.repeat(jnp.exp(steps), extent[dim] // shards_of).reshape((-1,) + (1,) * (len(extent) - 1 - dim))
    return loudness


def routed_block(rng, own, number, rows, number_of, top, limit, slope):
    ranking = jax.random.permutation(rng, number_of)
    heavy_load, ordinary = shares(number_of, rows * top, limit, slope, True), shares(number_of, rows * top, limit, slope, False)
    places = jnp.arange(number_of)

    def named(tallies, rotation):
        used = int((tallies > 0).sum())
        fixed = max(1, used // 4)
        moved = fixed + (places - fixed + rotation * (used - fixed)) % max(1, number_of - fixed)
        return jnp.zeros((number_of,), jnp.int32).at[ranking[jnp.where(places < fixed, places, moved)]].set(jnp.asarray(tallies, jnp.int32))

    tallies = jnp.where(number % 4 == 0, named(heavy_load, number // 4), named(ordinary, number - number // 4 - 1))
    mixed = jax.random.permutation(jax.random.fold_in(own, 3), number_of)
    donor, receiver = mixed[0:number_of // 2 * 2:2], mixed[1:number_of // 2 * 2:2]
    margin = jnp.minimum(tallies[donor] - 1, limit - tallies[receiver]) // 2
    margin = jnp.where((donor == ranking[0]) | (receiver == ranking[0]) | (tallies[receiver] == 0), 0, jnp.maximum(margin, 0))
    moved = jax.random.randint(jax.random.fold_in(own, 4), (number_of // 2,), 0, 1 << 20) % (margin + 1)
    tallies = tallies.at[donor].add(-moved).at[receiver].add(moved)
    items = jnp.searchsorted(jnp.cumsum(tallies), jnp.arange(rows * top), side="right").astype(jnp.int32)
    table = items.reshape(top, rows).T
    table = table[jax.random.permutation(jax.random.fold_in(own, 1), rows)]
    rotation = jax.random.randint(jax.random.fold_in(own, 2), (rows, 1), 0, top)
    return jnp.take_along_axis(table, (jnp.arange(top)[None, :] + rotation) % top, axis=1)


def shares(count, total, limit, skew, full):
    loads = [(1 << 20) // math.isqrt(rank ** skew) + 1 for rank in range(1, count + 1)]
    largest = limit if full else min(limit, max(-(-total // count), total * loads[0] // sum(loads)))
    least = 1 if total - largest >= count - 1 else 0
    given, spare = [largest] + [least] * (count - 1), total - largest - least * (count - 1)
    while spare > 0:
        candidates = [i for i in range(1, count) if given[i] < largest] or [i for i in range(1, count) if given[i] < limit]
        mass, remaining = sum([loads[i] for i in candidates]), spare
        for i in candidates:
            addition = min(limit - given[i], max(1, remaining * loads[i] // mass), spare)
            given[i] = given[i] + addition
            spare = spare - addition
    return np.array(given)


def gaussian(stream_key, dims, width, bound, pieces=(), held_as=jnp.bfloat16):
    level = steps_of(stream_key, dims, pieces, -0.22, 0.18) if pieces else 1.0
    array = jax.random.normal(stream_key, dims, jnp.float32) * width * level
    return jnp.minimum(jnp.maximum(array, -bound), bound).astype(held_as)


def setup_inputs(seed: int = 0) -> dict:
    keys = jax.random.split(jax.random.key(seed), 11)
    up_acts = gaussian(keys[0], (SECTIONS, TOKS, D), 1.0, 6.0, ((0, 8), (1, 16)))
    down_acts = gaussian(keys[1], (SECTIONS, TOKS, D), 1.0, 6.0, ((0, 8), (1, 16)))
    norm_gain = jnp.clip(1.0 + 0.18 * jax.random.normal(keys[2], (SECTIONS, D), jnp.float32), 0.1, 1.9)
    up_routes_keys = jax.random.split(jax.random.fold_in(keys[3], 1), SECTIONS * TOKS // TOK_DEV)
    up_routes_turns = jax.random.permutation(jax.random.fold_in(keys[3], 3), SECTIONS * TOKS // TOK_DEV)
    up_routes = jax.vmap(lambda own, number: routed_block(jax.random.fold_in(keys[3], 2), own, number, TOK_DEV, EXPERTS, TOPK, TOK_DEV, 2))(up_routes_keys, up_routes_turns).reshape((SECTIONS, TOKS, TOPK))
    down_routes_keys = jax.random.split(jax.random.fold_in(keys[4], 1), SECTIONS * TOKS // TOK_DEV)
    down_routes_turns = jax.random.permutation(jax.random.fold_in(keys[4], 3), SECTIONS * TOKS // TOK_DEV)
    down_routes = jax.vmap(lambda own, number: routed_block(jax.random.fold_in(keys[4], 2), own, number, TOK_DEV, EXPERTS, TOPK, TOK_DEV, 2))(down_routes_keys, down_routes_turns).reshape((SECTIONS, TOKS, TOPK))
    up_gates = jnp.clip(jnp.exp(math.log(1.0) - 1.609438 * jax.random.uniform(keys[5], (SECTIONS, TOKS, TOPK), jnp.float32) ** steps_of(keys[5], (SECTIONS, TOKS, TOPK), ((0, 8), (1, 16)), -0.2, 0.2)), 0.2, 1.0)
    down_gates = jnp.clip(jnp.exp(math.log(1.0) - 1.609438 * jax.random.uniform(keys[6], (SECTIONS, TOKS, TOPK), jnp.float32) ** steps_of(keys[6], (SECTIONS, TOKS, TOPK), ((0, 8), (1, 16)), -0.2, 0.2)), 0.2, 1.0)
    gate_weight = gaussian(keys[7], (SECTIONS, D, EXPERTS * FF), D ** -0.5, 0.09375, ((0, 8), (2, 16)))
    up_weight = gaussian(keys[8], (SECTIONS, D, EXPERTS * FF), D ** -0.5, 0.09375, ((0, 8), (2, 16)))
    down_weight = gaussian(keys[9], (SECTIONS, EXPERTS * FF, D), FF ** -0.5, 0.125, ((0, 8), (1, 16)))
    return {"up_acts": up_acts, "down_acts": down_acts, "norm_gain": norm_gain, "up_routes": up_routes, "down_routes": down_routes, "up_gates": up_gates, "down_gates": down_gates, "gate_weight": gate_weight, "up_weight": up_weight, "down_weight": down_weight}


def section_layer(activations, scaling, routes, gate_weights, gate_block, up_block, down_block):
    widened = activations.astype(jnp.float32)
    mean_square = lax.optimization_barrier(jnp.mean(widened * widened, axis=-1, keepdims=True))
    normed = (widened * lax.rsqrt(mean_square + 1e-06) * scaling[None, :]).astype(jnp.bfloat16)
    labels = jnp.arange(EXPERTS, dtype=jnp.int32)
    chosen = (routes[:, :, None] == labels[None, None, :]).astype(jnp.float32)
    mixing = lax.optimization_barrier(jnp.sum(gate_weights[:, :, None] * chosen, axis=1))
    combined = widened
    for expert in range(EXPERTS):
        accumulated = jnp.zeros(widened.shape, jnp.float32)
        for block in range(SPLIT):
            column_start = expert * FF + block * H_DEV
            gate_value = jnp.dot(normed, gate_block[:, column_start:column_start + H_DEV], preferred_element_type=jnp.float32)
            up_value = jnp.dot(normed, up_block[:, column_start:column_start + H_DEV], preferred_element_type=jnp.float32)
            hidden = (jax.nn.silu(gate_value) * up_value).astype(jnp.bfloat16)
            partial_value = jnp.dot(hidden, down_block[column_start:column_start + H_DEV], preferred_element_type=jnp.float32)
            partial_value = lax.optimization_barrier(partial_value.astype(jnp.bfloat16))
            accumulated = accumulated + partial_value.astype(jnp.float32)
        expert_out = lax.optimization_barrier(accumulated.astype(jnp.bfloat16))
        combined = combined + mixing[:, expert:expert + 1] * expert_out.astype(jnp.float32)
    return combined.astype(jnp.bfloat16)

def reference(up_acts, down_acts, norm_gain, up_routes, down_routes, up_gates, down_gates, gate_weight, up_weight, down_weight):
    upward = []
    downward = []
    for section in range(SECTIONS):
        upward.append(section_layer(up_acts[section], norm_gain[section], up_routes[section], up_gates[section], gate_weight[section], up_weight[section], down_weight[section]))
        downward.append(section_layer(down_acts[section], norm_gain[section], down_routes[section], down_gates[section], gate_weight[section], up_weight[section], down_weight[section]))
    next_up = jnp.stack(upward[-1:] + upward[:-1])
    next_down = jnp.stack(downward[1:] + downward[:1])
    return (next_up, next_down)
```

```python
import functools

import jax
import jax.numpy as jnp
from jax import lax
from jax.experimental import pallas as pl
from jax.experimental.pallas import tpu as pltpu
from jax.sharding import PartitionSpec as P

EXTRA = 128
TILE = 256


def place(y, z, c):
    return (y * 4 + z) * 2 + c


DEVICES = [(y, z, c) for y in range(2) for z in range(4) for c in range(2)]
CORE = [(place(y, z, c), place(y, z, 1 - c)) for y, z, c in DEVICES]
ACROSS = [(place(y, z, c), place(1 - y, z, c)) for y, z, c in DEVICES]
OUTWARD = [(place(y, z, c), place(y, (z + 1 - 2 * c) % 4, c)) for y, z, c in DEVICES]
HOMEWARD = [(place(y, z, c), place(y, (z - 1 + 2 * c) % 4, c)) for y, z, c in DEVICES]


def core(block):
    return lax.ppermute(block, "expert", CORE)


def across(block):
    return lax.ppermute(block, "expert", ACROSS)


def outward(block):
    return lax.ppermute(block, "expert", OUTWARD)


def homeward(block):
    return lax.ppermute(block, "expert", HOMEWARD)


def shifted(block, distance):
    devices = range(lax.axis_size("section"))
    route = [((i - distance) % len(devices), i) for i in devices]
    return lax.ppermute(block, "section", route)


def ffn_kernel(parts, width, *refs):
    x_refs = refs[:parts]
    mine = refs[parts : parts + 3]
    other = refs[parts + 3 : parts + 6]
    out_refs = refs[parts + 6 : 2 * parts + 6]
    x_all, mix_all, total = refs[2 * parts + 6 :]
    step = pl.program_id(0)
    half = pl.num_programs(0) // 2

    @pl.when(step == 0)
    def _():
        expert = lax.axis_index("expert") // 4
        row = 0
        for x_ref in x_refs:
            rows = x_ref.shape[0]
            x_all[row : row + rows, :] = x_ref[:, :width]
            tail = x_ref[:, width:].astype(jnp.float32)
            column = lax.broadcasted_iota(jnp.int32, tail.shape, 1)
            kept = jnp.where((column == expert) | (column == expert + 4), tail, 0.0)
            mix_all[row : row + rows, :] = jnp.sum(kept, axis=1, keepdims=True)
            row += rows

    def work(weights):
        gate_ref, up_ref, down_ref = weights
        x = x_all[...]
        gate_value = jnp.dot(x, gate_ref[...], preferred_element_type=jnp.float32)
        up_value = jnp.dot(x, up_ref[...], preferred_element_type=jnp.float32)
        hidden = gate_value * (1.0 / (1.0 + jnp.exp(-gate_value))) * up_value * mix_all[...]
        return jnp.dot(hidden.astype(jnp.bfloat16), down_ref[...], preferred_element_type=jnp.float32)

    @pl.when(step == 0)
    def _():
        total[...] = work(mine)

    @pl.when((step > 0) & (step < half))
    def _():
        total[...] += work(mine)

    @pl.when(step >= half)
    def _():
        total[...] += work(other)

    @pl.when(step == pl.num_programs(0) - 1)
    def _():
        row = 0
        for out_ref in out_refs:
            rows = out_ref.shape[0]
            out_ref[...] = total[row : row + rows, :].astype(out_ref.dtype)
            row += rows


def ffn(blocks, mine, other):
    width = mine[2].shape[1]
    units = mine[2].shape[0]
    rows = [block.shape[0] for block in blocks]
    total_rows = sum(rows)
    half = units // TILE

    def whole(count, columns):
        return pl.BlockSpec((count, columns), lambda j: (0, 0))

    def first(j):
        return jnp.minimum(j, half - 1)

    def second(j):
        return jnp.maximum(j - half, 0)

    def weight_specs(turn):
        return [
            pl.BlockSpec((width, TILE), lambda j: (0, turn(j))),
            pl.BlockSpec((width, TILE), lambda j: (0, turn(j))),
            pl.BlockSpec((TILE, width), lambda j: (turn(j), 0)),
        ]

    return pl.pallas_call(
        functools.partial(ffn_kernel, len(blocks), width),
        grid=(2 * half,),
        in_specs=[whole(r, width + EXTRA) for r in rows] + weight_specs(first) + weight_specs(second),
        out_specs=[whole(r, width) for r in rows],
        out_shape=[jax.ShapeDtypeStruct((r, width), jnp.bfloat16) for r in rows],
        scratch_shapes=[
            pltpu.VMEM((total_rows, width), jnp.bfloat16),
            pltpu.VMEM((total_rows, 1), jnp.float32),
            pltpu.VMEM((total_rows, width), jnp.float32),
        ],
        cost_estimate=pl.CostEstimate(
            flops=2 * total_rows * width * 2 * units * 3,
            bytes_accessed=2 * 3 * 2 * units * width + 4 * total_rows * width,
            transcendentals=total_rows * 2 * units,
        ),
        compiler_params=pltpu.CompilerParams(vmem_limit_bytes=58 * 1024 * 1024),
    )(*blocks, *mine, *other)


def prepare(activations, scaling, routes, gate_weights):
    widened = activations.astype(jnp.float32)
    mean_square = jnp.mean(widened * widened, axis=-1, keepdims=True)
    normed = (widened * lax.rsqrt(mean_square + 1e-06) * scaling[None, :]).astype(jnp.bfloat16)
    column = jnp.arange(EXTRA, dtype=jnp.int32)
    label = jnp.where(column < 8, column % 4, -1)
    mixing = jnp.zeros((activations.shape[0], EXTRA), jnp.float32)
    for k in range(routes.shape[1]):
        mixing += jnp.where(routes[:, k : k + 1] == label[None, :], gate_weights[:, k : k + 1], 0.0)
    coarse = lax.reduce_precision(mixing, 8, 7)
    tail = jnp.where(column[None, :] < 4, coarse, mixing - coarse).astype(jnp.bfloat16)
    return jnp.concatenate([normed, tail], axis=1)


def gather(own):
    rows = own.shape[0]
    beside = core(own)
    near = outward(jnp.concatenate([own, beside]))
    facing = across(own)
    facing_beside = core(facing)
    second = outward(jnp.concatenate([near[:rows], facing, facing_beside]))
    far, facing_near = second[:rows], second[rows:]
    facing_far = across(far)
    return (own, near, facing, far, facing_near, facing_far)


def add(*terms):
    total = terms[0].astype(jnp.float32)
    for term in terms[1:]:
        total = total + term.astype(jnp.float32)
    return total


def combine(activations, partials):
    own, near, facing, far, facing_near, facing_far = partials
    rows = own.shape[0]
    far = add(far, across(facing_far)).astype(jnp.bfloat16)
    back = homeward(jnp.concatenate([far, facing_near]))
    near = jnp.concatenate([add(near[:rows], back[:rows]).astype(jnp.bfloat16), near[rows:]])
    facing = add(facing, back[rows : 2 * rows], core(back[2 * rows :])).astype(jnp.bfloat16)
    last = homeward(near)
    crossed = across(facing)
    return add(activations, own, last[:rows], core(last[rows:]), crossed).astype(jnp.bfloat16)


def body(
    up_acts,
    down_acts,
    norm_gain,
    up_routes,
    down_routes,
    up_gates,
    down_gates,
    gate_weight,
    up_weight,
    down_weight,
):
    mine = (gate_weight[0], up_weight[0], down_weight[0])
    other = tuple(core(w) for w in mine)
    up_own = prepare(up_acts[0], norm_gain[0], up_routes[0], up_gates[0])
    down_own = prepare(down_acts[0], norm_gain[0], down_routes[0], down_gates[0])
    up_blocks = gather(up_own)
    down_blocks = gather(down_own)
    up_partials = ffn(up_blocks, mine, other)
    up_layer = combine(up_acts[0], up_partials)
    next_up = shifted(up_layer, 1)
    down_partials = ffn(down_blocks, mine, other)
    down_layer = combine(down_acts[0], down_partials)
    next_down = shifted(down_layer, -1)
    return (next_up[None], next_down[None])


def solution(mesh):
    return jax.shard_map(
        body,
        mesh=mesh,
        in_specs=(
            P("section", "expert", None),
            P("section", "expert", None),
            P("section", None),
            P("section", "expert", None),
            P("section", "expert", None),
            P("section", "expert", None),
            P("section", "expert", None),
            P("section", None, "expert"),
            P("section", None, "expert"),
            P("section", "expert", None),
        ),
        out_specs=(P("section", "expert", None), P("section", "expert", None)),
        check_vma=False,
    )
```

```python
import functools

import jax
import jax.numpy as jnp
from jax import lax
from jax.experimental import pallas as pl
from jax.experimental.pallas import tpu as pltpu
from jax.sharding import PartitionSpec as P

EXTRA = 128
TILE = 256
WIDE = 1792


def place(y, z, c):
    return (y * 4 + z) * 2 + c


DEVICES = [(y, z, c) for y in range(2) for z in range(4) for c in range(2)]
CORE = [(place(y, z, c), place(y, z, 1 - c)) for y, z, c in DEVICES]
ACROSS = [(place(y, z, c), place(1 - y, z, c)) for y, z, c in DEVICES]
OUTWARD = [(place(y, z, c), place(y, (z + 1 - 2 * c) % 4, c)) for y, z, c in DEVICES]
OPPOSITE = [(place(y, z, c), place(y, (z + 2) % 4, c)) for y, z, c in DEVICES]
CROSSING = [(place(y, z, c), place(y, (z - 1 + 2 * c) % 4, 1 - c)) for y, z, c in DEVICES]


def core(block):
    return lax.ppermute(block, "expert", CORE)


def across(block):
    return lax.ppermute(block, "expert", ACROSS)


def outward(block):
    return lax.ppermute(block, "expert", OUTWARD)


def crossing(block):
    return lax.ppermute(block, "expert", CROSSING)


def homeward(block):
    return lax.ppermute(block, "expert", [(target, source) for source, target in OUTWARD])


def recrossing(block):
    return lax.ppermute(block, "expert", [(target, source) for source, target in CROSSING])


def opposite(block):
    return lax.ppermute(block, "expert", OPPOSITE)


def shifted(block, distance):
    sections = lax.axis_size("section")
    route = [(i, (i + distance) % sections) for i in range(sections)]
    return lax.ppermute(block, "section", route)


def shifted_across(block, distance):
    sections, group = lax.axis_size("section"), len(DEVICES)
    route = [
        (i * group + source, (i + distance) % sections * group + target)
        for i in range(sections)
        for source, target in ACROSS
    ]
    return lax.ppermute(block, ("section", "expert"), route)


def ffn_kernel(parts, width, *refs):
    x_refs = refs[:parts]
    mine = refs[parts : parts + 3]
    other = refs[parts + 3 : parts + 6]
    out_refs = refs[parts + 6 : 2 * parts + 6]
    x_all, hidden_all = refs[2 * parts + 6 :]
    units = mine[2].shape[0]
    expert = lax.axis_index("expert") // 4
    shares = []
    row = 0
    for x_ref in x_refs:
        rows = x_ref.shape[0]
        x_all[row : row + rows, :] = x_ref[:, :width]
        tail = x_ref[:, width:].astype(jnp.float32)
        column = lax.broadcasted_iota(jnp.int32, tail.shape, 1)
        kept = jnp.where((column == expert) | (column == expert + 4), tail, 0.0)
        shares.append(jnp.sum(kept, axis=1, keepdims=True))
        row += rows
    share = jnp.concatenate(shares)
    for side, (gate_ref, up_ref, _) in enumerate((mine, other)):
        for start in range(0, units, TILE):
            x = x_all[...]
            columns = pl.ds(start, TILE)
            gate_value = jnp.dot(x, gate_ref[:, columns], preferred_element_type=jnp.float32)
            up_value = jnp.dot(x, up_ref[:, columns], preferred_element_type=jnp.float32)
            hidden = gate_value * (1.0 / (1.0 + jnp.exp(-gate_value))) * up_value * share
            hidden_all[:, pl.ds(side * units + start, TILE)] = hidden.astype(jnp.bfloat16)

    @pl.loop(0, width // WIDE)
    def _(n):
        columns = pl.ds(pl.multiple_of(n * WIDE, WIDE), WIDE)
        partial = jnp.dot(hidden_all[:, :units], mine[2][:, columns], preferred_element_type=jnp.float32)
        partial += jnp.dot(hidden_all[:, units:], other[2][:, columns], preferred_element_type=jnp.float32)
        row = 0
        for out_ref in out_refs:
            rows = out_ref.shape[0]
            out_ref[:, columns] = partial[row : row + rows].astype(out_ref.dtype)
            row += rows


def ffn(blocks, mine, other):
    units, width = mine[2].shape
    rows = [block.shape[0] for block in blocks]
    total_rows = sum(rows)
    vmem = pl.BlockSpec(memory_space=pltpu.VMEM)
    return pl.pallas_call(
        functools.partial(ffn_kernel, len(blocks), width),
        in_specs=[vmem] * (len(blocks) + 6),
        out_specs=[vmem] * len(blocks),
        out_shape=[jax.ShapeDtypeStruct((r, width), jnp.bfloat16) for r in rows],
        scratch_shapes=[
            pltpu.VMEM((total_rows, width), jnp.bfloat16),
            pltpu.VMEM((total_rows, 2 * units), jnp.bfloat16),
        ],
        cost_estimate=pl.CostEstimate(
            flops=2 * total_rows * width * 2 * units * 3,
            bytes_accessed=2 * 3 * 2 * units * width,
            transcendentals=total_rows * 2 * units,
        ),
        compiler_params=pltpu.CompilerParams(vmem_limit_bytes=14 * 1024 * 1024),
    )(*blocks, *mine, *other)


def prepare_kernel(acts_hbm, gain_hbm, routes_hbm, gates_hbm, out_ref, acts_ref, gain_ref, routes_ref, gates_ref, sems):
    pairs = ((routes_hbm, routes_ref), (gates_hbm, gates_ref), (gain_hbm, gain_ref), (acts_hbm, acts_ref))
    copies = [pltpu.make_async_copy(source, target, sems.at[i]) for i, (source, target) in enumerate(pairs)]
    for copy in copies:
        copy.start()
    for copy in copies:
        copy.wait()
    width = acts_ref.shape[1]
    widened = acts_ref[...].astype(jnp.float32)
    mean_square = jnp.mean(widened * widened, axis=-1, keepdims=True)
    normed = widened * lax.rsqrt(mean_square + 1e-06) * gain_ref[...]
    out_ref[:, :width] = normed.astype(jnp.bfloat16)
    rows = acts_ref.shape[0]
    label = lax.broadcasted_iota(jnp.int32, (EXTRA, rows), 0)
    expert = jnp.where(label < 8, label % 4, -1)
    mixing = jnp.zeros(label.shape, jnp.float32)
    for k in range(routes_ref.shape[0]):
        mixing += jnp.where(routes_ref[k : k + 1, :] == expert, gates_ref[k : k + 1, :], 0.0)
    coarse = mixing.astype(jnp.bfloat16).astype(jnp.float32)
    tail = jnp.where(label < 4, coarse, mixing - coarse)
    out_ref[:, width:] = tail.T.astype(jnp.bfloat16)


def prepare(activations, gain, routes, gate_weights):
    rows, width = activations.shape
    arrays = (activations, gain, routes.T, gate_weights.T)
    return pl.pallas_call(
        prepare_kernel,
        in_specs=[pl.BlockSpec(memory_space=pltpu.HBM)] * 4,
        out_specs=pl.BlockSpec(memory_space=pltpu.VMEM),
        out_shape=jax.ShapeDtypeStruct((rows, width + EXTRA), jnp.bfloat16),
        scratch_shapes=[pltpu.VMEM(array.shape, array.dtype) for array in arrays] + [pltpu.SemaphoreType.DMA((4,))],
        cost_estimate=pl.CostEstimate(flops=6 * rows * width, bytes_accessed=4 * rows * width, transcendentals=rows),
        compiler_params=pltpu.CompilerParams(vmem_limit_bytes=8 * 1024 * 1024),
    )(*arrays)


def after(block, *earlier):
    return lax.optimization_barrier((block, *earlier))[0]


def add(*terms):
    total = terms[0].astype(jnp.float32)
    for term in terms[1:]:
        total = total + term.astype(jnp.float32)
    return total.astype(jnp.bfloat16)


def first_step(own):
    return across(own), outward(own), crossing(own)


def second_step(facing, near, beside):
    facing, near, beside = lax.optimization_barrier((facing, near, beside))
    rows = facing.shape[0]
    ahead = outward(jnp.concatenate([near, facing]))
    facing_beside = crossing(facing)
    return ahead[:rows], ahead[rows:], facing_beside


def combine(activations, close, distant, last, distance):
    own, near, beside, facing = close
    far, facing_near, facing_beside = distant
    rows = own.shape[0]
    far = add(far, across(last))
    ahead = homeward(jnp.concatenate([far, facing_near]))
    near = add(near, ahead[:rows])
    facing = add(facing, ahead[rows:], recrossing(facing_beside))
    near, facing, beside = lax.optimization_barrier((near, facing, beside))
    crossed = shifted_across(facing, distance)
    layer = add(activations, own, homeward(near), recrossing(beside))
    return add(shifted(layer, distance), crossed)


def body(
    up_acts,
    down_acts,
    norm_gain,
    up_routes,
    down_routes,
    up_gates,
    down_gates,
    gate_weight,
    up_weight,
    down_weight,
):
    mine = (gate_weight[0], up_weight[0], down_weight[0])
    other = tuple(core(w) for w in mine)
    up_own = prepare(up_acts[0], norm_gain, up_routes[0], up_gates[0])
    down_own = prepare(down_acts[0], norm_gain, down_routes[0], down_gates[0])
    run = functools.partial(ffn, mine=mine, other=other)
    up_facing, up_near, up_beside = first_step(up_own)
    down_facing, down_near, down_beside = first_step(down_own)
    up_distant = second_step(up_facing, up_near, up_beside)
    up_close = run((up_own, up_near, up_beside, up_facing))
    down_distant = second_step(after(down_facing, up_close[0]), down_near, down_beside)
    down_close = run((down_own, down_near, down_beside, down_facing))
    up_last = across(after(up_distant[0], down_close[0]))
    up_distant = run(up_distant)
    down_last = across(after(down_distant[0], up_distant[0]))
    down_distant = run(down_distant)
    (up_last,) = run((after(up_last, down_distant[0]),))
    (down_last,) = run((after(down_last, up_last),))
    next_up = combine(up_acts[0], up_close, up_distant, up_last, 1)
    next_down = combine(down_acts[0], down_close, down_distant, down_last, -1)
    return (next_up[None], next_down[None])


def solution(mesh):
    return jax.shard_map(
        body,
        mesh=mesh,
        in_specs=(
            P("section", "expert", None),
            P("section", "expert", None),
            P("section", None),
            P("section", "expert", None),
            P("section", "expert", None),
            P("section", "expert", None),
            P("section", "expert", None),
            P("section", None, "expert"),
            P("section", None, "expert"),
            P("section", "expert", None),
        ),
        out_specs=(P("section", "expert", None), P("section", "expert", None)),
        check_vma=False,
    )
```

```python
import functools

import jax
import jax.numpy as jnp
from jax import lax
from jax.experimental import pallas as pl
from jax.experimental.pallas import tpu as pltpu
from jax.sharding import PartitionSpec as P

EXTRA = 128
TILE = 256
WIDE = 1792


def place(y, z, c):
    return (y * 4 + z) * 2 + c


DEVICES = [(y, z, c) for y in range(2) for z in range(4) for c in range(2)]
CORE = [(place(y, z, c), place(y, z, 1 - c)) for y, z, c in DEVICES]
ACROSS = [(place(y, z, c), place(1 - y, z, c)) for y, z, c in DEVICES]
OUTWARD = [(place(y, z, c), place(y, (z + 1 - 2 * c) % 4, c)) for y, z, c in DEVICES]
CROSSING = [(place(y, z, c), place(y, (z - 1 + 2 * c) % 4, 1 - c)) for y, z, c in DEVICES]
OPPOSITE = [(place(y, z, c), place(y, (z + 2) % 4, c)) for y, z, c in DEVICES]


def sent(route):
    return lambda block: lax.ppermute(block, "expert", route)


def inverse(route):
    return [(target, source) for source, target in route]


core, across, opposite = sent(CORE), sent(ACROSS), sent(OPPOSITE)
outward, crossing = sent(OUTWARD), sent(CROSSING)
homeward, recrossing = sent(inverse(OUTWARD)), sent(inverse(CROSSING))


def shifted(block, distance):
    sections = lax.axis_size("section")
    route = [(i, (i + distance) % sections) for i in range(sections)]
    return lax.ppermute(block, "section", route)


def shifted_across(block, distance):
    sections, group = lax.axis_size("section"), len(DEVICES)
    route = [
        (i * group + source, (i + distance) % sections * group + target)
        for i in range(sections)
        for source, target in ACROSS
    ]
    return lax.ppermute(block, ("section", "expert"), route)


def ffn_kernel(parts, width, *refs):
    x_refs = refs[:parts]
    mine = refs[parts : parts + 3]
    other = refs[parts + 3 : parts + 6]
    out_refs = refs[parts + 6 : -2]
    x_all, hidden_all = refs[-2:]
    units = mine[2].shape[0]
    expert = lax.axis_index("expert") // 4
    shares = []
    row = 0
    for x_ref in x_refs:
        rows = x_ref.shape[0]
        x_all[row : row + rows, :] = x_ref[:, :width]
        tail = x_ref[:, width:].astype(jnp.float32)
        column = lax.broadcasted_iota(jnp.int32, tail.shape, 1)
        kept = jnp.where((column == expert) | (column == expert + 4), tail, 0.0)
        shares.append(jnp.sum(kept, axis=1, keepdims=True))
        row += rows
    share = jnp.concatenate(shares)
    for side, (gate_ref, up_ref, _) in enumerate((mine, other)):
        for start in range(0, units, TILE):
            x = x_all[...]
            columns = pl.ds(start, TILE)
            gate_value = jnp.dot(x, gate_ref[:, columns], preferred_element_type=jnp.float32)
            up_value = jnp.dot(x, up_ref[:, columns], preferred_element_type=jnp.float32)
            hidden = gate_value * (1.0 / (1.0 + jnp.exp(-gate_value))) * up_value * share
            hidden_all[:, pl.ds(side * units + start, TILE)] = hidden.astype(jnp.bfloat16)

    @pl.loop(0, width // WIDE)
    def _(n):
        columns = pl.ds(pl.multiple_of(n * WIDE, WIDE), WIDE)
        partial = jnp.dot(hidden_all[:, :units], mine[2][:, columns], preferred_element_type=jnp.float32)
        partial += jnp.dot(hidden_all[:, units:], other[2][:, columns], preferred_element_type=jnp.float32)
        row = 0
        for out_ref in out_refs:
            rows = out_ref.shape[0]
            out_ref[:, columns] = partial[row : row + rows].astype(out_ref.dtype)
            row += rows


def ffn(*blocks, weights):
    mine, other = weights[:3], weights[3:]
    units, width = mine[2].shape
    results = [block.shape[0] for block in blocks]
    total_rows = sum(block.shape[0] for block in blocks)
    vmem = pl.BlockSpec(memory_space=pltpu.VMEM)
    return pl.pallas_call(
        functools.partial(ffn_kernel, len(blocks), width),
        in_specs=[vmem] * (len(blocks) + 6),
        out_specs=[vmem] * len(results),
        out_shape=[jax.ShapeDtypeStruct((r, width), jnp.bfloat16) for r in results],
        scratch_shapes=[
            pltpu.VMEM((total_rows, width), jnp.bfloat16),
            pltpu.VMEM((total_rows, 2 * units), jnp.bfloat16),
        ],
        cost_estimate=pl.CostEstimate(
            flops=2 * total_rows * width * 2 * units * 3,
            bytes_accessed=2 * 3 * 2 * units * width,
            transcendentals=total_rows * 2 * units,
        ),
        compiler_params=pltpu.CompilerParams(vmem_limit_bytes=14 * 1024 * 1024),
    )(*blocks, *mine, *other)


def prepare_kernel(*refs):
    count = len(refs) // 2 - 1
    sources, out_ref, targets, sems = refs[:count], refs[count], refs[count + 1 : -1], refs[-1]
    copies = [pltpu.make_async_copy(sources[i], targets[i], sems.at[i]) for i in range(count)]
    for copy in copies:
        copy.start()
    for copy in copies:
        copy.wait()
    acts_ref, gain_ref, routes_ref, gates_ref = targets
    rows, width = acts_ref.shape
    widened = acts_ref[...].astype(jnp.float32)
    mean_square = jnp.mean(widened * widened, axis=-1, keepdims=True)
    normed = widened * lax.rsqrt(mean_square + 1e-06) * gain_ref[...]
    out_ref[:, :width] = normed.astype(jnp.bfloat16)
    label = lax.broadcasted_iota(jnp.int32, (EXTRA, rows), 0)
    expert = jnp.where(label < 8, label % 4, -1)
    mixing = jnp.zeros(label.shape, jnp.float32)
    for k in range(routes_ref.shape[0]):
        mixing += jnp.where(routes_ref[k : k + 1, :] == expert, gates_ref[k : k + 1, :], 0.0)
    coarse = mixing.astype(jnp.bfloat16).astype(jnp.float32)
    tail = jnp.where(label < 4, coarse, mixing - coarse)
    out_ref[:, width:] = tail.T.astype(jnp.bfloat16)


def prepare(activations, gain, routes, gate_weights):
    rows, width = activations.shape
    arrays = (activations, gain, routes.T, gate_weights.T)
    return pl.pallas_call(
        prepare_kernel,
        in_specs=[pl.BlockSpec(memory_space=pltpu.HBM)] * len(arrays),
        out_specs=pl.BlockSpec(memory_space=pltpu.VMEM),
        out_shape=jax.ShapeDtypeStruct((rows, width + EXTRA), jnp.bfloat16),
        scratch_shapes=[pltpu.VMEM(array.shape, array.dtype) for array in arrays]
        + [pltpu.SemaphoreType.DMA((len(arrays),))],
        cost_estimate=pl.CostEstimate(flops=6 * rows * width, bytes_accessed=4 * rows * width, transcendentals=rows),
        compiler_params=pltpu.CompilerParams(vmem_limit_bytes=60 * 1024 * 1024),
    )(*arrays)


def after(block, *earlier):
    return lax.optimization_barrier((block, *[e[0] if isinstance(e, (tuple, list)) else e for e in earlier]))[0]


def add(*terms):
    total = terms[0].astype(jnp.float32)
    for term in terms[1:]:
        total = total + term.astype(jnp.float32)
    return total.astype(jnp.bfloat16)


def body(
    up_acts,
    down_acts,
    norm_gain,
    up_routes,
    down_routes,
    up_gates,
    down_gates,
    gate_weight,
    up_weight,
    down_weight,
):
    up_acts, up_routes, up_gates = up_acts[0], up_routes[0], up_gates[0]
    down_acts, down_routes, down_gates = down_acts[0], down_routes[0], down_gates[0]
    gate_weight, up_weight, down_weight = gate_weight[0], up_weight[0], down_weight[0]
    down_rows = prepare(down_acts, norm_gain, down_routes, down_gates)
    up_rows = prepare(after(up_acts, down_rows), norm_gain, up_routes, up_gates)
    other_gate = core(after(gate_weight, up_rows))
    other_down = core(after(down_weight, up_rows))
    up_near = outward(up_rows)
    up_far = outward(up_near)
    down_near = outward(down_rows)
    other_up = core(after(up_weight, other_gate, other_down, down_near))
    up_facing = across(after(up_rows, other_down, down_near))
    down_facing = across(after(down_rows, up_rows, down_near))
    down_facing_beside = crossing(after(down_facing, other_up))
    down_far = outward(down_near)
    up_facing_beside = crossing(after(up_facing, other_up, down_far, down_facing))
    up_facing_far = across(after(up_far, other_up, down_far, down_facing))
    down_facing_near = outward(after(down_facing, other_gate, up_near, other_down, down_near))
    up_facing_near = outward(after(up_facing, down_facing_near, up_far, other_up, down_far))
    down_beside = crossing(after(down_rows, up_facing_far, up_facing_near))
    down_facing_far = across(after(down_far, down_facing, other_gate, other_down, other_up))
    run = functools.partial(ffn, weights=(gate_weight, up_weight, down_weight, other_gate, other_up, other_down))
    down_distant = run(down_far, down_facing_near, down_facing_beside)
    up_beside = crossing(after(up_rows, up_facing_beside, down_distant, down_facing_far))
    down_last = run(after(down_facing_far, up_facing_beside, down_distant))
    up_distant = run(after(up_far, down_last, up_facing_far), up_facing_near, up_facing_beside)
    up_last = run(after(up_facing_far, up_beside, up_distant))
    up_last_back = across(after(up_last, down_beside)[0])
    down_last_back = across(after(down_last, up_facing_far, up_facing_near)[0])
    down_facing_beside_back = recrossing(after(down_distant, down_facing_far)[2])
    up_facing_beside_back = recrossing(after(up_distant, down_facing_beside_back)[2])
    up_facing_near_back = homeward(after(up_distant, up_beside, down_facing_beside_back)[1])
    down_close = run(after(down_rows, up_facing_beside_back, down_last_back, up_last), down_near, down_beside, down_facing)
    up_close = run(after(up_rows, down_close), up_near, up_beside, up_facing)
    down_far_back = opposite(add(after(down_distant, up_last, down_beside)[0], down_last_back))
    up_facing_out = shifted_across(add(after(up_close, down_far_back, up_last_back)[3], up_facing_near_back, up_facing_beside_back), 1)
    up_far_back = homeward(add(after(up_distant, up_close, down_far_back)[0], up_last_back))
    down_near_back = homeward(after(down_close, up_facing_near_back)[1])
    down_beside_back = recrossing(down_close[2])
    up_beside_back = recrossing(after(up_close, down_beside_back, down_far_back, up_last_back)[2])
    up_near_back = homeward(add(after(up_close, down_near_back, down_beside_back)[1], up_far_back))
    down_facing_near_back = homeward(after(down_distant, down_beside_back, up_close, down_far_back, up_last_back)[1])
    down_facing_out = shifted_across(add(after(down_close, up_facing_out, up_beside_back, down_near_back)[3], down_facing_near_back, down_facing_beside_back), -1)
    down_layer = shifted(add(after(down_acts, up_close, up_last_back), down_close[0], down_near_back, down_beside_back, down_far_back), -1)
    up_layer = shifted(add(after(up_acts, down_layer, down_facing_near_back, up_facing_out), up_close[0], up_near_back, up_beside_back), 1)
    down_next = add(down_layer, down_facing_out)
    up_next = add(after(up_layer, down_next), up_facing_out)
    return (up_next[None], down_next[None])


def solution(mesh):
    return jax.shard_map(
        body,
        mesh=mesh,
        in_specs=(
            P("section", "expert", None),
            P("section", "expert", None),
            P("section", None),
            P("section", "expert", None),
            P("section", "expert", None),
            P("section", "expert", None),
            P("section", "expert", None),
            P("section", None, "expert"),
            P("section", None, "expert"),
            P("section", "expert", None),
        ),
        out_specs=(P("section", "expert", None), P("section", "expert", None)),
        check_vma=False,
    )
```

```python
import functools

import jax
import jax.numpy as jnp
from jax import lax
from jax.experimental import pallas as pl
from jax.experimental.pallas import tpu as pltpu
from jax.sharding import PartitionSpec as P

EXTRA = 128
TILE = 256
WIDE = 1792


def place(y, z, c):
    return (y * 4 + z) * 2 + c


DEVICES = [(y, z, c) for y in range(2) for z in range(4) for c in range(2)]
CORE = [(place(y, z, c), place(y, z, 1 - c)) for y, z, c in DEVICES]
ACROSS = [(place(y, z, c), place(1 - y, z, c)) for y, z, c in DEVICES]
OUTWARD = [(place(y, z, c), place(y, (z + 1 - 2 * c) % 4, c)) for y, z, c in DEVICES]
CROSSING = [(place(y, z, c), place(y, (z - 1 + 2 * c) % 4, 1 - c)) for y, z, c in DEVICES]
OPPOSITE = [(place(y, z, c), place(y, (z + 2) % 4, c)) for y, z, c in DEVICES]


def sent(route):
    return lambda block: lax.ppermute(block, "expert", route)


def inverse(route):
    return [(target, source) for source, target in route]


core, across, opposite = sent(CORE), sent(ACROSS), sent(OPPOSITE)
outward, crossing = sent(OUTWARD), sent(CROSSING)
homeward, recrossing = sent(inverse(OUTWARD)), sent(inverse(CROSSING))


def shifted(block, distance):
    sections = lax.axis_size("section")
    route = [(i, (i + distance) % sections) for i in range(sections)]
    return lax.ppermute(block, "section", route)


def shifted_across(block, distance):
    sections, group = lax.axis_size("section"), len(DEVICES)
    route = [
        (i * group + source, (i + distance) % sections * group + target)
        for i in range(sections)
        for source, target in ACROSS
    ]
    return lax.ppermute(block, ("section", "expert"), route)


def ffn_kernel(parts, width, *refs):
    x_refs = refs[:parts]
    mine = refs[parts : parts + 3]
    other = refs[parts + 3 : parts + 6]
    out_refs = refs[parts + 6 : -2]
    x_all, hidden_all = refs[-2:]
    units = mine[2].shape[0]
    expert = lax.axis_index("expert") // 4
    shares = []
    row = 0
    for x_ref in x_refs:
        rows = x_ref.shape[0]
        x_all[row : row + rows, :] = x_ref[:, :width]
        tail = x_ref[:, width:].astype(jnp.float32)
        column = lax.broadcasted_iota(jnp.int32, tail.shape, 1)
        kept = jnp.where((column == expert) | (column == expert + 4), tail, 0.0)
        shares.append(jnp.sum(kept, axis=1, keepdims=True))
        row += rows
    share = jnp.concatenate(shares)
    for side, (gate_ref, up_ref, _) in enumerate((mine, other)):
        for start in range(0, units, TILE):
            x = x_all[...]
            columns = pl.ds(start, TILE)
            gate_value = jnp.dot(x, gate_ref[:, columns], preferred_element_type=jnp.float32)
            up_value = jnp.dot(x, up_ref[:, columns], preferred_element_type=jnp.float32)
            hidden = gate_value * (1.0 / (1.0 + jnp.exp(-gate_value))) * up_value * share
            hidden_all[:, pl.ds(side * units + start, TILE)] = hidden.astype(jnp.bfloat16)

    for start in range(0, width, WIDE):
        columns = pl.ds(start, WIDE)
        partial = jnp.dot(hidden_all[:, :units], mine[2][:, columns], preferred_element_type=jnp.float32)
        partial += jnp.dot(hidden_all[:, units:], other[2][:, columns], preferred_element_type=jnp.float32)
        row = 0
        for out_ref in out_refs:
            rows = out_ref.shape[0]
            out_ref[:, columns] = partial[row : row + rows].astype(out_ref.dtype)
            row += rows


def ffn(*blocks, weights):
    mine, other = weights[:3], weights[3:]
    units, width = mine[2].shape
    results = [block.shape[0] for block in blocks]
    total_rows = sum(block.shape[0] for block in blocks)
    vmem = pl.BlockSpec(memory_space=pltpu.VMEM)
    return pl.pallas_call(
        functools.partial(ffn_kernel, len(blocks), width),
        in_specs=[vmem] * (len(blocks) + 6),
        out_specs=[vmem] * len(results),
        out_shape=[jax.ShapeDtypeStruct((r, width), jnp.bfloat16) for r in results],
        scratch_shapes=[
            pltpu.VMEM((total_rows, width), jnp.bfloat16),
            pltpu.VMEM((total_rows, 2 * units), jnp.bfloat16),
        ],
        cost_estimate=pl.CostEstimate(
            flops=2 * total_rows * width * 2 * units * 3,
            bytes_accessed=2 * 3 * 2 * units * width,
            transcendentals=total_rows * 2 * units,
        ),
        compiler_params=pltpu.CompilerParams(vmem_limit_bytes=14 * 1024 * 1024),
    )(*blocks, *mine, *other)


def prepare_kernel(*refs):
    count = len(refs) // 2 - 1
    sources, out_ref, targets, sems = refs[:count], refs[count], refs[count + 1 : -1], refs[-1]
    copies = [pltpu.make_async_copy(sources[i], targets[i], sems.at[i]) for i in range(count)]
    for copy in copies:
        copy.start()
    for copy in copies:
        copy.wait()
    acts_ref, gain_ref, routes_ref, gates_ref = targets
    rows, width = acts_ref.shape
    widened = acts_ref[...].astype(jnp.float32)
    mean_square = jnp.mean(widened * widened, axis=-1, keepdims=True)
    normed = widened * lax.rsqrt(mean_square + 1e-06) * gain_ref[...]
    out_ref[:, :width] = normed.astype(jnp.bfloat16)
    label = lax.broadcasted_iota(jnp.int32, (EXTRA, rows), 0)
    expert = jnp.where(label < 8, label % 4, -1)
    mixing = jnp.zeros(label.shape, jnp.float32)
    for k in range(routes_ref.shape[0]):
        mixing += jnp.where(routes_ref[k : k + 1, :] == expert, gates_ref[k : k + 1, :], 0.0)
    coarse = mixing.astype(jnp.bfloat16).astype(jnp.float32)
    tail = jnp.where(label < 4, coarse, mixing - coarse)
    out_ref[:, width:] = tail.T.astype(jnp.bfloat16)


def prepare(activations, gain, routes, gate_weights):
    rows, width = activations.shape
    arrays = (activations, gain, routes.T, gate_weights.T)
    return pl.pallas_call(
        prepare_kernel,
        in_specs=[pl.BlockSpec(memory_space=pltpu.HBM)] * len(arrays),
        out_specs=pl.BlockSpec(memory_space=pltpu.VMEM),
        out_shape=jax.ShapeDtypeStruct((rows, width + EXTRA), jnp.bfloat16),
        scratch_shapes=[pltpu.VMEM(array.shape, array.dtype) for array in arrays]
        + [pltpu.SemaphoreType.DMA((len(arrays),))],
        cost_estimate=pl.CostEstimate(flops=6 * rows * width, bytes_accessed=4 * rows * width, transcendentals=rows),
        compiler_params=pltpu.CompilerParams(vmem_limit_bytes=60 * 1024 * 1024),
    )(*arrays)


def after(block, *earlier):
    return lax.optimization_barrier((block, *[e[0] if isinstance(e, (tuple, list)) else e for e in earlier]))[0]


def add(*terms):
    total = terms[0].astype(jnp.float32)
    for term in terms[1:]:
        total = total + term.astype(jnp.float32)
    return total.astype(jnp.bfloat16)


def body(
    up_acts,
    down_acts,
    norm_gain,
    up_routes,
    down_routes,
    up_gates,
    down_gates,
    gate_weight,
    up_weight,
    down_weight,
):
    up_acts, up_routes, up_gates = up_acts[0], up_routes[0], up_gates[0]
    down_acts, down_routes, down_gates = down_acts[0], down_routes[0], down_gates[0]
    gate_weight, up_weight, down_weight = gate_weight[0], up_weight[0], down_weight[0]
    down_rows = prepare(down_acts, norm_gain, down_routes, down_gates)
    up_rows = prepare(after(up_acts, down_rows), norm_gain, up_routes, up_gates)
    other_gate = core(after(gate_weight, up_rows))
    other_down = core(after(down_weight, up_rows))
    up_near = outward(up_rows)
    up_far = outward(up_near)
    down_near = outward(down_rows)
    other_up = core(after(up_weight, other_gate, other_down, down_near))
    up_facing = across(after(up_rows, other_down, down_near))
    down_facing = across(after(down_rows, up_rows, down_near))
    down_facing_beside = crossing(after(down_facing, other_up))
    down_far = outward(down_near)
    up_facing_beside = crossing(after(up_facing, other_up, down_far, down_facing))
    up_facing_far = across(after(up_far, other_up, down_far, down_facing))
    down_facing_near = outward(after(down_facing, other_gate, up_near, other_down, down_near))
    up_facing_near = outward(after(up_facing, down_facing_near, up_far, other_up, down_far))
    down_beside = crossing(after(down_rows, up_facing_far, up_facing_near))
    down_facing_far = across(after(down_far, down_facing, other_gate, other_down, other_up))
    run = functools.partial(ffn, weights=(gate_weight, up_weight, down_weight, other_gate, other_up, other_down))
    down_distant = run(down_far, down_facing_near, down_facing_beside)
    up_beside = crossing(after(up_rows, up_facing_beside, down_distant, down_facing_far))
    down_last = run(after(down_facing_far, up_facing_beside, down_distant))
    up_distant = run(after(up_far, down_last, up_facing_far), up_facing_near, up_facing_beside)
    up_last = run(after(up_facing_far, up_beside, up_distant))
    up_last_back = across(after(up_last, down_beside)[0])
    down_last_back = across(after(down_last, up_facing_far, up_facing_near)[0])
    down_facing_beside_back = recrossing(after(down_distant, down_facing_far)[2])
    up_facing_beside_back = recrossing(after(up_distant, down_facing_beside_back)[2])
    up_facing_near_back = homeward(after(up_distant, up_beside, down_facing_beside_back)[1])
    down_close = run(after(down_rows, up_facing_beside_back, down_last_back, up_last), down_near, down_beside, down_facing)
    up_close = run(after(up_rows, down_close), up_near, up_beside, up_facing)
    down_far_back = opposite(add(after(down_distant, up_last, down_beside)[0], down_last_back))
    up_facing_out = shifted_across(add(after(up_close, down_far_back, up_last_back)[3], up_facing_near_back, up_facing_beside_back), 1)
    up_far_back = homeward(add(after(up_distant, up_close, down_far_back)[0], up_last_back))
    down_near_back = homeward(after(down_close, up_facing_near_back)[1])
    down_beside_back = recrossing(down_close[2])
    up_beside_back = recrossing(after(up_close, down_beside_back, down_far_back, up_last_back)[2])
    up_near_back = homeward(add(after(up_close, down_near_back, down_beside_back)[1], up_far_back))
    down_facing_near_back = homeward(after(down_distant, down_beside_back, up_close, down_far_back, up_last_back)[1])
    down_facing_out = shifted_across(add(after(down_close, up_facing_out, up_beside_back, down_near_back)[3], down_facing_near_back, down_facing_beside_back), -1)
    down_layer = shifted(add(after(down_acts, up_close, up_last_back), down_close[0], down_near_back, down_beside_back, down_far_back), -1)
    up_layer = shifted(add(after(up_acts, down_layer, down_facing_near_back, up_facing_out), up_close[0], up_near_back, up_beside_back), 1)
    down_next = add(down_layer, down_facing_out)
    up_next = add(after(up_layer, down_next), up_facing_out)
    return (up_next[None], down_next[None])


def solution(mesh):
    return jax.shard_map(
        body,
        mesh=mesh,
        in_specs=(
            P("section", "expert", None),
            P("section", "expert", None),
            P("section", None),
            P("section", "expert", None),
            P("section", "expert", None),
            P("section", "expert", None),
            P("section", "expert", None),
            P("section", None, "expert"),
            P("section", None, "expert"),
            P("section", "expert", None),
        ),
        out_specs=(P("section", "expert", None), P("section", "expert", None)),
        check_vma=False,
    )
```
